128 devices in a mesh: orb: 16 (over x, z), aux: 8 (over y, core).
Axes of the slice: x: 4, y: 4, z: 4, core: 2. Of those that a mesh axis runs over, the one named last changes fastest.
Arguments:
- three_center: bfloat16 [16, 4, 128, 128, 128], P('orb', None, 'aux'), may hold values from -0.25 to 0.25
- density: bfloat16 [2048, 2048], P('aux'), may hold values from -6 to 6
- pattern: int32 [16, 4], replicated, may hold values from 0 to 15, as said below
- counts: int32 [16], replicated, may hold values from 1 to 4, as said below
- order: int32 [16], replicated, may hold values from 0 to 15, each once
Outputs:
- exchange: float32 [2048, 2048], P('orb', 'aux')
The draws below stay inside these ranges and needn't reach their ends.
Inputs may be any that keep to these rules, and one draw needn't show every extreme that they name: Each row of pattern lists 4 different blocks. `counts`: some row block has all 4 slots live. `order`: a permutation of the 16 row blocks.
All inputs are finite; a program needn't handle non-finite values.
Results may differ from the reference program's by a relative error of at most 0.0029.
Values may be sent and summed in bfloat16 or wider, within the bound.
No kernel may reach another device: no remote copies, remote signals or barrier semaphores. Data moves between devices by JAX's collectives and lax.ppermute only.
A program may use at most 192 MiB of HBM per device.

```python
import jax
import jax.numpy as jnp
from jax import lax

BLK = 128
NZ = 4
NB = 16
NAUX = 128
NBF = 2048


def draw_pattern(key, part):
    key = jax.random.fold_in(key, 11)
    keys = jax.random.split(key, NB)
    offsets = jax.vmap(lambda single: jax.random.permutation(single, NB))(keys)[:, :NZ]
    return ((jnp.arange(NB)[:, None] + offsets) % NB).astype(jnp.int32)


def draw_counts(key, part):
    key = jax.random.fold_in(key, 12)
    first, second = jax.random.split(key)
    drawn = jax.random.randint(first, (NB,), 1, NZ + 1)
    fullest = jax.random.randint(second, (), 0, NB)
    return jnp.where(jnp.arange(NB) == fullest, NZ, drawn).astype(jnp.int32)


def block_levels(own_key, shape, cuts, least, largest):
    gain = 1.0
    for dim, parts in cuts:
        draws = jax.random.uniform(jax.random.fold_in(jax.random.fold_in(own_key, 6), dim), (parts,), jnp.float32, least / len(cuts), largest / len(cuts))
        gain = gain * jnp.repeat(jnp.exp(draws), shape[dim] // parts).reshape((-1,) + (1,) * (len(shape) - 1 - dim))
    return gain


def noise(key, extent, spread, bound, shards=(), kind=jnp.bfloat16):
    gain = block_levels(key, extent, shards, -0.22, 0.18) if shards else 1.0
    array = jax.random.normal(key, extent, jnp.float32) * spread * gain
    return jnp.minimum(jnp.maximum(array, -bound), bound).astype(kind)


def setup_inputs(seed: int = 0) -> dict:
    seeds = jax.random.split(jax.random.key(seed), 6)
    return {
        "three_center": noise(seeds[0], (NB, NZ, NAUX, BLK, BLK), (NZ * BLK) ** -0.5, 0.25, ((0, 16), (2, 8))),
        "density": noise(seeds[1], (NBF, NBF), 1.0, 6.0, ((0, 8),)),
        "pattern": draw_pattern(jax.random.fold_in(seeds[5], 71), 0),
        "counts": draw_counts(jax.random.fold_in(seeds[5], 71), 0),
        "order": jax.random.permutation(seeds[4], NB).astype(jnp.int32),
    }


def reference(three_center, density, pattern, counts, order):
    blocks = pattern.shape[0]
    tensor = three_center.astype(jnp.float32)
    keep_live = jnp.arange(NZ)[None, :] < counts[:, None]
    masked = jnp.where(keep_live[:, :, None, None, None], tensor, jnp.float32(0.0))
    dense = density.astype(jnp.float32).reshape(blocks, BLK, blocks * BLK)

    def one_row(owner):
        chosen = jnp.take(dense, pattern[owner], axis=0)
        product = jnp.einsum('kpab,kbs->pas', masked[owner], chosen, precision=lax.Precision.HIGHEST)
        product = lax.optimization_barrier(product.astype(jnp.bfloat16)).astype(jnp.float32)
        halfway_grid = product.reshape(NAUX, BLK, blocks, BLK)
        selected = jnp.take(halfway_grid, pattern, axis=2)
        return jnp.einsum('pankc,nkpbc->nab', selected, masked, precision=lax.Precision.HIGHEST)

    raw = lax.map(one_row, jnp.arange(blocks, dtype=jnp.int32))
    factor = jnp.float32(0.5 / (NAUX ** 0.5))
    symmetric = (raw + jnp.transpose(raw, (1, 0, 3, 2))) * factor
    inverse = jnp.argsort(order).astype(jnp.int32)
    natural = jnp.take(symmetric, inverse, axis=1)
    return natural.transpose(0, 2, 1, 3).reshape(blocks * BLK, blocks * BLK)
```

```python
import functools
import math

import jax
import jax.numpy as jnp
from jax import lax
from jax.experimental import pallas as pl
from jax.experimental.pallas import tpu as pltpu
from jax.sharding import Mesh
from jax.sharding import PartitionSpec as P

W = 128
HALF = 8
KEEP = 5


def pair_kernel(pattern, counts, core, own, other, dens, out, half_ref, raw_ref):
    blocks, depth = own.shape[0], own.shape[1]
    both = (own, other)

    def operand(j, k, count):
        live = (k < count).astype(jnp.float32).astype(jnp.bfloat16)
        return [ref[j, k] * live for ref in both]

    def halfway_row(j, _):
        count = counts[j]
        rows = pl.ds(pl.multiple_of(j * W, W), W)

        def run(slots):
            left = [operand(j, k, count) for k in range(slots)]
            left = jnp.concatenate([jnp.concatenate(pair, axis=0) for pair in left], axis=1)
            step = 4 * W
            for n in range(blocks // 4):
                right = jnp.concatenate(
                    [dens[pattern[j, k], :, n * step : (n + 1) * step] for k in range(slots)], axis=0
                )
                product = jnp.dot(left, right, preferred_element_type=jnp.float32)
                product = product.astype(jnp.bfloat16)
                for s in range(4):
                    for p in range(2):
                        half_ref[p, n * 4 + s, rows, :] = product[
                            p * W : (p + 1) * W, s * W : (s + 1) * W
                        ]

        @pl.when(count <= 2)
        def _():
            run(2)

        @pl.when(count > 2)
        def _():
            run(depth)

        return 0

    lax.fori_loop(0, blocks, halfway_row, 0)

    def raw_column(i, _):
        count = counts[i]
        side = jnp.bitwise_xor(i // HALF, core[0])
        base = pl.multiple_of(side * (HALF * W), HALF * W)

        def run(slots):
            right = [operand(i, k, count) for k in range(slots)]
            right = jnp.concatenate([jnp.concatenate(pair, axis=1) for pair in right], axis=1)
            step = 2 * W
            for m in range(HALF // 2):
                rows = pl.ds(pl.multiple_of(base + m * step, step), step)
                left = jnp.concatenate(
                    [half_ref[p, pattern[i, k], rows, :] for k in range(slots) for p in range(2)],
                    axis=1,
                )
                raw_ref[i, m * step : (m + 1) * step, :] = lax.dot_general(
                    left, right, (((1,), (1,)), ((), ())), preferred_element_type=jnp.float32
                )

        @pl.when(count <= 2)
        def _():
            run(2)

        @pl.when(count > 2)
        def _():
            run(depth)

        return 0

    lax.fori_loop(0, blocks, raw_column, 0)

    def collect(j, _):
        here, side = j % HALF, jnp.bitwise_xor(j // HALF, core[0])
        for q in range(KEEP):
            there = (here + q) % HALF
            i = side * HALF + there
            first = raw_ref[i, pl.ds(pl.multiple_of(here * W, W), W), :]
            second = raw_ref[j, pl.ds(pl.multiple_of(there * W, W), W), :]
            out[j, q] = (first + second.T).astype(out.dtype)
        return 0

    lax.fori_loop(0, blocks, collect, 0)


def partial_blocks(pattern, counts, core, own, other, dens):
    blocks = own.shape[0]
    smem = pl.BlockSpec(memory_space=pltpu.SMEM)
    vmem = pl.BlockSpec(memory_space=pltpu.VMEM)
    return pl.pallas_call(
        pair_kernel,
        out_shape=jax.ShapeDtypeStruct((blocks, KEEP, W, W), jnp.bfloat16),
        in_specs=[smem, smem, smem, vmem, vmem, vmem],
        out_specs=vmem,
        scratch_shapes=[
            pltpu.VMEM((2, blocks, blocks * W, W), jnp.bfloat16),
            pltpu.VMEM((blocks, HALF * W, W), jnp.float32),
        ],
        compiler_params=pltpu.CompilerParams(vmem_limit_bytes=56 * 2**20),
        cost_estimate=pl.CostEstimate(flops=13 * 10**9, bytes_accessed=15 * 2**20, transcendentals=0),
        name="pair_blocks",
    )(pattern, counts, core, own, other, dens)


def swap_core(array, parts):
    pieces = jnp.split(array, parts, axis=0)
    moved = [lax.ppermute(piece, "core", [(0, 1), (1, 0)]) for piece in pieces]
    return jnp.concatenate(moved, axis=0)


def per_device(three_center, density, pattern, counts, order):
    blocks = pattern.shape[0]
    core = lax.axis_index("core")
    here_y = lax.axis_index("y")
    outgoing = jnp.swapaxes(three_center[0], 0, 1)
    own = lax.all_to_all(outgoing, ("x", "z"), 0, 0, tiled=True)
    other = swap_core(own, 4)
    dens = lax.all_gather(density, ("y", "core"), axis=0, tiled=True)
    dens = dens.reshape(blocks, W, blocks * W)
    partial = partial_blocks(pattern, counts, core.reshape(1).astype(jnp.int32), own, other, dens)
    arrived = lax.all_to_all(partial, ("x", "z"), 0, 0, tiled=True)
    kept = jnp.sum(arrived.astype(jnp.float32), axis=0)
    mirrored = []
    for q in (3, 2, 1):
        route = []
        for j in range(blocks):
            for c in range(2):
                partner = HALF * ((j // HALF) ^ c) + (j % HALF + q) % HALF
                route.append((j * 2 + c, partner * 2 + c))
        block = lax.ppermute(kept[q], ("x", "z", "core"), route)
        mirrored.append(block.T)
    mine = jnp.concatenate([kept, jnp.stack(mirrored)], axis=0)
    orb = lax.axis_index("x") * 4 + lax.axis_index("z")
    theirs = swap_core(mine, 2)
    inverse = jnp.argsort(order)
    offset = (inverse - orb) % HALF
    side = (inverse // HALF) ^ (orb // HALF)
    from_own = (side == core)
    index = jnp.where(from_own, offset, offset + HALF)
    pool = jnp.concatenate([mine, theirs], axis=0)
    index = index.reshape(4, 2, 2)
    index = lax.dynamic_index_in_dim(index, core, 1, keepdims=False)

    def chunk(d):
        wanted = lax.dynamic_index_in_dim(index, (here_y + d) % 4, 0, keepdims=False)
        return jnp.take(pool, wanted, axis=0)

    total = chunk(0)
    for d in (2, 1, 3):
        total = total + lax.ppermute(chunk(d), "y", [(y, (y + d) % 4) for y in range(4)])
    factor = jnp.float32(0.5 / math.sqrt(three_center.shape[2] * lax.axis_size("y") * lax.axis_size("core")))
    return (total * factor).transpose(1, 0, 2).reshape(W, 2 * W)


def solution(mesh):
    fine = Mesh(mesh.devices.reshape(4, 4, 4, 2), ("x", "z", "y", "core"))
    rows, cols = ("x", "z"), ("y", "core")
    return jax.shard_map(
        per_device,
        mesh=fine,
        in_specs=(P(rows, None, cols, None, None), P(cols, None), P(), P(), P()),
        out_specs=P(rows, cols),
        check_vma=False,
    )
```

```python
import functools
import math

import jax
import jax.numpy as jnp
from jax import lax
from jax.experimental import pallas as pl
from jax.experimental.pallas import tpu as pltpu
from jax.sharding import Mesh
from jax.sharding import PartitionSpec as P

W = 128
HALF = 8
KEEP = 5
H_GROUP, R_GROUP = 4, 4
PARTS = 2
SHIFTS = (0, 0, -1, -1, 1, 1, 2, 2)


def pair_kernel(info, *refs):
    pieces, (out, half_ref, direct, turned, both, dens, ranked, sems, dens_sems) = refs[:-9], refs[-9:]
    _, blocks, depth = both.shape[:3]
    core, here_y = lax.axis_index("core"), lax.axis_index("y")

    def live(j, k):
        return info[blocks * depth + j] > k

    def operand(j, k):
        keep = live(j, k).astype(jnp.float32).astype(jnp.bfloat16)
        return [both[p, j, k] * keep for p in range(2)]

    early, first = [], 0
    for piece in pieces:
        if len(piece.shape) == 4:
            p, at = first // blocks, first % blocks
            early.append(pltpu.make_async_copy(piece, both.at[p, pl.ds(at, piece.shape[0])], sems.at[len(early)]))
            first += piece.shape[0]
    rows = []
    for piece in pieces:
        if len(piece.shape) == 2:
            rows += [piece.at[pl.ds(r, W)] for r in range(0, piece.shape[0], W)]
    part = blocks * W // PARTS

    def dens_copy(n, at):
        c, rest = divmod(at, blocks // 2)
        place = 4 * lax.rem(here_y + SHIFTS[rest] + 4, 4) + 2 * jnp.bitwise_xor(core, c) + rest % 2
        cols = pl.ds(pl.multiple_of(n * part, part), part)
        return pltpu.make_async_copy(rows[at].at[:, cols], dens.at[place, :, cols], dens_sems.at[n, at])

    for copy in early:
        copy.start()
    for n in range(PARTS):
        for at in range(blocks):
            dens_copy(n, at).start()

    def place(j, at, slots):
        hit = info[blocks * depth + j] == slots

        @pl.when(hit)
        def _():
            ranked[at] = j

        return at + hit.astype(jnp.int32)

    filled = 0
    for slots in range(depth, 0, -1):
        filled = lax.fori_loop(0, blocks, functools.partial(place, slots=slots), filled)
    for copy in early:
        copy.wait()

    def halfway_part(n, _):
        for at in range(blocks):
            dens_copy(n, at).wait()

        def halfway_rows(g, _):
            group = [ranked[g * H_GROUP + t] for t in range(H_GROUP)]

            def run(slots):
                for j in group:
                    where = pl.ds(pl.multiple_of(j * W, W), W)
                    left = [operand(j, k) for k in range(slots)]
                    left = jnp.concatenate([jnp.concatenate(pair, axis=0) for pair in left], axis=1)
                    step = 4 * W
                    for m in range(part // step):
                        cols = pl.ds(pl.multiple_of(n * part + m * step, step), step)
                        right = jnp.concatenate([dens[info[j * depth + k], :, cols] for k in range(slots)], axis=0)
                        product = jnp.dot(left, right, preferred_element_type=jnp.float32)
                        product = product.astype(jnp.bfloat16)
                        for s in range(step // W):
                            for p in range(2):
                                half_ref[p, n * (part // W) + m * (step // W) + s, where, :] = product[
                                    p * W : (p + 1) * W, s * W : (s + 1) * W
                                ]

            @pl.when(jnp.logical_not(live(group[0], 2)))
            def _():
                run(2)

            @pl.when(live(group[0], 2))
            def _():
                run(depth)

            return 0

        return lax.fori_loop(0, blocks // H_GROUP, halfway_rows, 0)

    lax.fori_loop(0, PARTS, halfway_part, 0)

    def raw_columns(g, _):
        group = [ranked[g * R_GROUP + t] for t in range(R_GROUP)]

        def run(slots):
            for i in group:
                raw_column(i, slots)

        for slots in range(1, depth + 1):

            @pl.when(info[blocks * depth + group[0]] == slots)
            def _(slots=slots):
                run(slots)

        return 0

    def raw_column(i, slots):
        there = lax.rem(i, HALF)
        side = jnp.bitwise_xor(i // HALF, core)
        right = jnp.concatenate([x for k in range(slots) for x in operand(i, k)], axis=1)
        for m in range(0, HALF, 2):
            rows_of = [side * HALF + lax.rem(there + r, HALF) for r in (m, m + 1)]
            left = [
                jnp.concatenate(
                    [
                        half_ref[p, info[i * depth + k], pl.ds(pl.multiple_of(j * W, W), W), :]
                        for k in range(slots)
                        for p in range(2)
                    ],
                    axis=1,
                )
                for j in rows_of
            ]
            raw = lax.dot_general(
                jnp.concatenate(left, axis=0), right, (((1,), (1,)), ((), ())),
                preferred_element_type=jnp.float32,
            )
            for r, j in zip((m, m + 1), rows_of):
                block = raw[(r - m) * W : (r - m + 1) * W, :]
                if (-r) % HALF < KEEP:
                    direct[j, (-r) % HALF] = block
                if r < KEEP:
                    turned[i, r] = block.T

    lax.fori_loop(0, blocks // R_GROUP, raw_columns, 0)

    def collect(j, _):
        out[j] = (direct[j] + turned[j]).astype(out.dtype)
        return 0

    lax.fori_loop(0, blocks, collect, 0)


def partial_blocks(info, blocks, depth, *pieces):
    return pl.pallas_call(
        pair_kernel,
        out_shape=jax.ShapeDtypeStruct((blocks, KEEP, W, W), jnp.bfloat16),
        in_specs=[pl.BlockSpec(memory_space=pltpu.SMEM)] + [pl.BlockSpec(memory_space=pl.ANY)] * len(pieces),
        out_specs=pl.BlockSpec(memory_space=pltpu.VMEM),
        scratch_shapes=[
            pltpu.VMEM((2, blocks, blocks * W, W), jnp.bfloat16),
            pltpu.VMEM((blocks, KEEP, W, W), jnp.float32),
            pltpu.VMEM((blocks, KEEP, W, W), jnp.float32),
            pltpu.VMEM((2, blocks, depth, W, W), jnp.bfloat16),
            pltpu.VMEM((blocks, W, blocks * W), jnp.bfloat16),
            pltpu.SMEM((blocks,), jnp.int32),
            pltpu.SemaphoreType.DMA((len(pieces),)),
            pltpu.SemaphoreType.DMA((PARTS, blocks)),
        ],
        compiler_params=pltpu.CompilerParams(vmem_limit_bytes=58 * 2**20),
        cost_estimate=pl.CostEstimate(flops=13 * 10**9, bytes_accessed=15 * 2**20, transcendentals=0),
        name="pair_blocks",
    )(info, *pieces)


def reorder_kernel(source, target, held, sems):
    copies = [pltpu.make_async_copy(source.at[k], held.at[:, k], sems.at[k]) for k in range(source.shape[0])]
    for copy in copies:
        copy.start()
    for copy in copies:
        copy.wait()
    last = pltpu.make_async_copy(held, target, sems.at[source.shape[0]])
    last.start()
    last.wait()


def by_function(blocks):
    depth, functions = blocks.shape[:2]
    shape = (functions, depth, W, W)
    return pl.pallas_call(
        reorder_kernel,
        out_shape=jax.ShapeDtypeStruct(shape, blocks.dtype),
        in_specs=[pl.BlockSpec(memory_space=pl.ANY)],
        out_specs=pl.BlockSpec(memory_space=pl.ANY),
        scratch_shapes=[pltpu.VMEM(shape, blocks.dtype), pltpu.SemaphoreType.DMA((depth + 1,))],
        cost_estimate=pl.CostEstimate(flops=0, bytes_accessed=4 * 2**20, transcendentals=0),
        name="by_function",
    )(blocks)


def swap_core(pieces):
    return [lax.ppermute(piece, "core", [(0, 1), (1, 0)]) for piece in pieces]


def turn(piece, step):
    return lax.ppermute(piece, "y", [(y, (y + step) % 4) for y in range(4)])


def per_device(three_center, density, pattern, counts, order):
    blocks = pattern.shape[0]
    core = lax.axis_index("core")
    here_y = lax.axis_index("y")
    low, high = density[:W], density[W:]
    low_up, high_down = turn(low, 1), turn(high, -1)
    high_up, low_down = turn(high, 1), turn(low, -1)
    low_far, high_far = turn(low_up, 1), turn(high_down, -1)
    rows = [density, low_up, high_up, low_down, high_down, low_far, high_far]
    outgoing = by_function(three_center[0])
    own = lax.all_to_all(outgoing, ("x", "z"), 0, 0, tiled=True)
    first = swap_core([density, low_up, high_down])
    own, first, low_down, high_up = lax.optimization_barrier((own, first, low_down, high_up))
    second = swap_core([high_up, low_down])
    other = swap_core(jnp.split(own, 4, axis=0))
    other, second, far = lax.optimization_barrier((other, second, rows[5:]))
    near = [first[0], first[1], second[0], second[1], first[2]] + swap_core(far)
    info = jnp.concatenate([pattern.reshape(-1), counts]).astype(jnp.int32)
    partial = partial_blocks(info, *pattern.shape, own, *other, *rows, *near)
    arrived = lax.all_to_all(partial, ("x", "z"), 0, 0, tiled=True)
    kept = jnp.sum(arrived.astype(jnp.float32), axis=0)
    mirrored = []
    for q in (3, 2, 1):
        route = []
        for j in range(blocks):
            for c in range(2):
                partner = HALF * ((j // HALF) ^ c) + (j % HALF + q) % HALF
                route.append((j * 2 + c, partner * 2 + c))
        block = lax.ppermute(kept[q], ("x", "z", "core"), route)
        mirrored.append(block.T)
    mine = jnp.concatenate([kept, jnp.stack(mirrored)], axis=0)
    orb = lax.axis_index("x") * 4 + lax.axis_index("z")
    theirs = jnp.concatenate(swap_core(jnp.split(mine, 2, axis=0)), axis=0)
    inverse = jnp.argsort(order)
    offset = (inverse - orb) % HALF
    side = (inverse // HALF) ^ (orb // HALF)
    from_own = (side == core)
    index = jnp.where(from_own, offset, offset + HALF)
    pool = jnp.concatenate([mine, theirs], axis=0)
    index = index.reshape(4, 2, 2)
    index = lax.dynamic_index_in_dim(index, core, 1, keepdims=False)

    def chunk(d):
        wanted = lax.dynamic_index_in_dim(index, (here_y + d) % 4, 0, keepdims=False)
        return jnp.take(pool, wanted, axis=0)

    total = chunk(0)
    for d in (2, 1, 3):
        total = total + lax.ppermute(chunk(d), "y", [(y, (y + d) % 4) for y in range(4)])
    factor = jnp.float32(0.5 / math.sqrt(three_center.shape[2] * lax.axis_size("y") * lax.axis_size("core")))
    return (total * factor).transpose(1, 0, 2).reshape(W, 2 * W)


def solution(mesh):
    fine = Mesh(mesh.devices.reshape(4, 4, 4, 2), ("x", "z", "y", "core"))
    rows, cols = ("x", "z"), ("y", "core")
    return jax.shard_map(
        per_device,
        mesh=fine,
        in_specs=(P(rows, None, cols, None, None), P(cols, None), P(), P(), P()),
        out_specs=P(rows, cols),
        check_vma=False,
    )
```

```python
import functools
import math

import jax
import jax.numpy as jnp
from jax import lax
from jax.experimental import pallas as pl
from jax.experimental.pallas import tpu as pltpu
from jax.sharding import Mesh
from jax.sharding import PartitionSpec as P

W = 128
HALF = 8
KEEP = 5
H_GROUP, R_GROUP = 4, 4
PARTS = 2
SHIFTS = (0, 0, -1, -1, 1, 1, 2, 2)


def pair_kernel(info, *refs):
    pieces, (half_ref, direct, turned, both, dens, ranked, sems, dens_sems) = refs[:-16], refs[-8:]
    outs = refs[-16:-8]
    _, blocks, depth = both.shape[:3]
    core, here_y = lax.axis_index("core"), lax.axis_index("y")

    def live(j, k):
        return info[blocks * depth + j] > k

    def operand(j, k):
        keep = live(j, k).astype(jnp.float32).astype(jnp.bfloat16)
        return [both[p, j, k] * keep for p in range(2)]

    early, first = [], 0
    for piece in pieces:
        if len(piece.shape) == 4:
            p, at = first // blocks, first % blocks
            early.append(pltpu.make_async_copy(piece, both.at[p, pl.ds(at, piece.shape[0])], sems.at[len(early)]))
            first += piece.shape[0]
    rows = []
    for piece in pieces:
        if len(piece.shape) == 2:
            rows += [piece.at[pl.ds(r, W)] for r in range(0, piece.shape[0], W)]
    part = blocks * W // PARTS

    def dens_copy(n, at):
        c, rest = divmod(at, blocks // 2)
        place = 4 * lax.rem(here_y + SHIFTS[rest] + 4, 4) + 2 * jnp.bitwise_xor(core, c) + rest % 2
        cols = pl.ds(pl.multiple_of(n * part, part), part)
        return pltpu.make_async_copy(rows[at].at[:, cols], dens.at[place, :, cols], dens_sems.at[n, at])

    for copy in early:
        copy.start()
    for n in range(PARTS):
        for at in range(blocks):
            dens_copy(n, at).start()

    def place(j, at, slots):
        hit = info[blocks * depth + j] == slots

        @pl.when(hit)
        def _():
            ranked[at] = j

        return at + hit.astype(jnp.int32)

    filled = 0
    for slots in range(depth, 0, -1):
        filled = lax.fori_loop(0, blocks, functools.partial(place, slots=slots), filled)
    for copy in early:
        copy.wait()

    def halfway_part(n, _):
        for at in range(blocks):
            dens_copy(n, at).wait()

        def halfway_rows(g, _):
            group = [ranked[g * H_GROUP + t] for t in range(H_GROUP)]

            def run(slots):
                for j in group:
                    where = pl.ds(pl.multiple_of(j * W, W), W)
                    left = [operand(j, k) for k in range(slots)]
                    left = jnp.concatenate([jnp.concatenate(pair, axis=0) for pair in left], axis=1)
                    step = 4 * W
                    for m in range(part // step):
                        cols = pl.ds(pl.multiple_of(n * part + m * step, step), step)
                        right = jnp.concatenate([dens[info[j * depth + k], :, cols] for k in range(slots)], axis=0)
                        product = jnp.dot(left, right, preferred_element_type=jnp.float32)
                        product = product.astype(jnp.bfloat16)
                        for s in range(step // W):
                            for p in range(2):
                                half_ref[p, n * (part // W) + m * (step // W) + s, where, :] = product[
                                    p * W : (p + 1) * W, s * W : (s + 1) * W
                                ]

            @pl.when(jnp.logical_not(live(group[0], 2)))
            def _():
                run(2)

            @pl.when(live(group[0], 2))
            def _():
                run(depth)

            return 0

        return lax.fori_loop(0, blocks // H_GROUP, halfway_rows, 0)

    lax.fori_loop(0, PARTS, halfway_part, 0)

    def raw_columns(g, _):
        group = [ranked[g * R_GROUP + t] for t in range(R_GROUP)]

        def run(slots):
            for i in group:
                raw_column(i, slots)

        for slots in range(1, depth + 1):

            @pl.when(info[blocks * depth + group[0]] == slots)
            def _(slots=slots):
                run(slots)

        return 0

    def raw_column(i, slots):
        there = lax.rem(i, HALF)
        side = jnp.bitwise_xor(i // HALF, core)
        right = jnp.concatenate([x for k in range(slots) for x in operand(i, k)], axis=1)
        for m in range(0, HALF, 2):
            rows_of = [side * HALF + lax.rem(there + r, HALF) for r in (m, m + 1)]
            left = [
                jnp.concatenate(
                    [
                        half_ref[p, info[i * depth + k], pl.ds(pl.multiple_of(j * W, W), W), :]
                        for k in range(slots)
                        for p in range(2)
                    ],
                    axis=1,
                )
                for j in rows_of
            ]
            raw = lax.dot_general(
                jnp.concatenate(left, axis=0), right, (((1,), (1,)), ((), ())),
                preferred_element_type=jnp.float32,
            )
            for r, j in zip((m, m + 1), rows_of):
                block = raw[(r - m) * W : (r - m + 1) * W, :]
                if (-r) % HALF < KEEP:
                    q = (-r) % HALF
                    direct[j, q * W : (q + 1) * W, :] = block
                if r < KEEP:
                    turned[i, r * W : (r + 1) * W, :] = block.T

    lax.fori_loop(0, blocks // R_GROUP, raw_columns, 0)

    here = (lax.axis_index("x"), lax.axis_index("z"))
    split = KEEP * W // 2

    def collect(other, _):
        for d in range(4):
            j = 4 * lax.rem(here[0] + d, 4) + other
            outs[d][other] = (direct[j, :split] + turned[j, :split]).astype(jnp.bfloat16)
            j = 4 * other + lax.rem(here[1] + d, 4)
            outs[4 + d][other] = (direct[j, split:] + turned[j, split:]).astype(jnp.bfloat16)
        return 0

    lax.fori_loop(0, 4, collect, 0)


def partial_blocks(info, blocks, depth, *pieces):
    return pl.pallas_call(
        pair_kernel,
        out_shape=[jax.ShapeDtypeStruct((4, KEEP * W // 2, W), jnp.bfloat16)] * 8,
        in_specs=[pl.BlockSpec(memory_space=pltpu.SMEM)] + [pl.BlockSpec(memory_space=pl.ANY)] * len(pieces),
        out_specs=[pl.BlockSpec(memory_space=pltpu.VMEM)] * 8,
        scratch_shapes=[
            pltpu.VMEM((2, blocks, blocks * W, W), jnp.bfloat16),
            pltpu.VMEM((blocks, KEEP * W, W), jnp.float32),
            pltpu.VMEM((blocks, KEEP * W, W), jnp.float32),
            pltpu.VMEM((2, blocks, depth, W, W), jnp.bfloat16),
            pltpu.VMEM((blocks, W, blocks * W), jnp.bfloat16),
            pltpu.SMEM((blocks,), jnp.int32),
            pltpu.SemaphoreType.DMA((len(pieces),)),
            pltpu.SemaphoreType.DMA((PARTS, blocks)),
        ],
        compiler_params=pltpu.CompilerParams(vmem_limit_bytes=58 * 2**20),
        cost_estimate=pl.CostEstimate(flops=13 * 10**9, bytes_accessed=15 * 2**20, transcendentals=0),
        name="pair_blocks",
    )(info, *pieces)


def reorder_kernel(source, target, held, sems):
    copies = [pltpu.make_async_copy(source.at[k], held.at[:, k], sems.at[k]) for k in range(source.shape[0])]
    for copy in copies:
        copy.start()
    for copy in copies:
        copy.wait()
    last = pltpu.make_async_copy(held, target, sems.at[source.shape[0]])
    last.start()
    last.wait()


def by_function(blocks):
    depth, functions = blocks.shape[:2]
    shape = (functions, depth, W, W)
    return pl.pallas_call(
        reorder_kernel,
        out_shape=jax.ShapeDtypeStruct(shape, blocks.dtype),
        in_specs=[pl.BlockSpec(memory_space=pl.ANY)],
        out_specs=pl.BlockSpec(memory_space=pl.ANY),
        scratch_shapes=[pltpu.VMEM(shape, blocks.dtype), pltpu.SemaphoreType.DMA((depth + 1,))],
        cost_estimate=pl.CostEstimate(flops=0, bytes_accessed=4 * 2**20, transcendentals=0),
        name="by_function",
    )(blocks)


def swap_core(pieces):
    return [lax.ppermute(piece, "core", [(0, 1), (1, 0)]) for piece in pieces]


def turn(piece, step):
    return lax.ppermute(piece, "y", [(y, (y + step) % 4) for y in range(4)])


def turn_on(axis, piece, step):
    return lax.ppermute(piece, axis, [(at, (at + step) % 4) for at in range(4)])


def exchange(sets):
    got = {}
    for d in (1, 3, 2):
        for n, (axis, pieces) in enumerate(sets):
            got[n, d] = turn_on(axis, pieces[d], d)
    return [
        pieces[0].astype(jnp.float32) + sum(got[n, d].astype(jnp.float32) for d in (1, 3, 2))
        for n, (_, pieces) in enumerate(sets)
    ]


def ahead(axis, array):
    at = lax.axis_index(axis)
    return [lax.dynamic_index_in_dim(array, (at + d) % 4, 0, keepdims=False) for d in range(4)]


def per_device(three_center, density, pattern, counts, order):
    blocks = pattern.shape[0]
    core = lax.axis_index("core")
    here_y = lax.axis_index("y")
    low, high = density[:W], density[W:]
    low_up, high_down = turn(low, 1), turn(high, -1)
    high_up, low_down = turn(high, 1), turn(low, -1)
    low_far, high_far = turn(low_up, 1), turn(high_down, -1)
    rows = [density, low_up, high_up, low_down, high_down, low_far, high_far]
    outgoing = by_function(three_center[0])
    own = lax.all_to_all(outgoing, ("x", "z"), 0, 0, tiled=True)
    first = swap_core([density, low_up, high_down])
    own, first, low_down, high_up = lax.optimization_barrier((own, first, low_down, high_up))
    second = swap_core([high_up, low_down])
    other = swap_core(jnp.split(own, 4, axis=0))
    other, second, far = lax.optimization_barrier((other, second, rows[5:]))
    near = [first[0], first[1], second[0], second[1], first[2]] + swap_core(far)
    info = jnp.concatenate([pattern.reshape(-1), counts]).astype(jnp.int32)
    partial = partial_blocks(info, *pattern.shape, own, *other, *rows, *near)
    first, second = exchange([("x", partial[:4]), ("z", partial[4:])])
    sets = [(axis, [piece.astype(jnp.bfloat16) if d else piece for d, piece in enumerate(ahead(axis, array))])
            for axis, array in (("z", first), ("x", second))]
    kept = jnp.concatenate(exchange(sets), axis=0).reshape(KEEP, W, W)
    mirrored = []
    for q in (3, 2, 1):
        route = []
        for j in range(blocks):
            for c in range(2):
                partner = HALF * ((j // HALF) ^ c) + (j % HALF + q) % HALF
                route.append((j * 2 + c, partner * 2 + c))
        block = lax.ppermute(kept[q], ("x", "z", "core"), route)
        mirrored.append(block.T)
    mine = jnp.concatenate([kept, jnp.stack(mirrored)], axis=0)
    orb = lax.axis_index("x") * 4 + lax.axis_index("z")
    theirs = jnp.concatenate(swap_core(jnp.split(mine, 2, axis=0)), axis=0)
    inverse = jnp.argsort(order)
    offset = (inverse - orb) % HALF
    side = (inverse // HALF) ^ (orb // HALF)
    from_own = (side == core)
    index = jnp.where(from_own, offset, offset + HALF)
    pool = jnp.concatenate([mine, theirs], axis=0)
    index = index.reshape(4, 2, 2)
    index = lax.dynamic_index_in_dim(index, core, 1, keepdims=False)

    def chunk(d):
        wanted = lax.dynamic_index_in_dim(index, (here_y + d) % 4, 0, keepdims=False)
        return jnp.take(pool, wanted, axis=0)

    total = chunk(0)
    for d in (2, 1, 3):
        total = total + lax.ppermute(chunk(d), "y", [(y, (y + d) % 4) for y in range(4)])
    factor = jnp.float32(0.5 / math.sqrt(three_center.shape[2] * lax.axis_size("y") * lax.axis_size("core")))
    return (total * factor).transpose(1, 0, 2).reshape(W, 2 * W)


def solution(mesh):
    fine = Mesh(mesh.devices.reshape(4, 4, 4, 2), ("x", "z", "y", "core"))
    rows, cols = ("x", "z"), ("y", "core")
    return jax.shard_map(
        per_device,
        mesh=fine,
        in_specs=(P(rows, None, cols, None, None), P(cols, None), P(), P(), P()),
        out_specs=P(rows, cols),
        check_vma=False,
    )
```

```python
import functools
import math

import jax
import jax.numpy as jnp
from jax import lax
from jax.experimental import pallas as pl
from jax.experimental.pallas import tpu as pltpu
from jax.sharding import Mesh
from jax.sharding import PartitionSpec as P

W = 128
HALF = 8
KEEP = 5
H_GROUP, R_GROUP = 8, 4
PARTS = 1
SHIFTS = (0, 0, -1, -1, 1, 1, 2, 2)


def pair_kernel(info, *refs):
    pieces, (half_ref, direct, turned, both, dens, ranked, sems, dens_sems) = refs[:-16], refs[-8:]
    outs = refs[-16:-8]
    _, blocks, depth = both.shape[:3]
    core, here_y = lax.axis_index("core"), lax.axis_index("y")

    def live(j, k):
        return info[blocks * depth + j] > k

    def operand(j, k):
        keep = live(j, k).astype(jnp.float32).astype(jnp.bfloat16)
        return [both[p, j, k] * keep for p in range(2)]

    early, first = [], 0
    for piece in pieces:
        if len(piece.shape) == 4:
            p, at = first // blocks, first % blocks
            early.append(pltpu.make_async_copy(piece, both.at[p, pl.ds(at, piece.shape[0])], sems.at[len(early)]))
            first += piece.shape[0]
    rows = []
    for piece in pieces:
        if len(piece.shape) == 2:
            rows += [piece.at[pl.ds(r, W)] for r in range(0, piece.shape[0], W)]
    part = blocks * W // PARTS

    def dens_copy(n, at):
        c, rest = divmod(at, blocks // 2)
        place = 4 * lax.rem(here_y + SHIFTS[rest] + 4, 4) + 2 * jnp.bitwise_xor(core, c) + rest % 2
        cols = pl.ds(pl.multiple_of(n * part, part), part)
        return pltpu.make_async_copy(rows[at].at[:, cols], dens.at[place, :, cols], dens_sems.at[n, at])

    for copy in early:
        copy.start()
    for n in range(PARTS):
        for at in range(blocks):
            dens_copy(n, at).start()

    def place(j, at, slots):
        hit = info[blocks * depth + j] == slots

        @pl.when(hit)
        def _():
            ranked[at] = j

        return at + hit.astype(jnp.int32)

    filled = 0
    for slots in range(depth, 0, -1):
        filled = lax.fori_loop(0, blocks, functools.partial(place, slots=slots), filled)
    for copy in early:
        copy.wait()

    def halfway_part(n, _):
        for at in range(blocks):
            dens_copy(n, at).wait()

        def halfway_rows(g, _):
            group = [ranked[g * H_GROUP + t] for t in range(H_GROUP)]

            def run(slots):
                for j in group:
                    where = pl.ds(pl.multiple_of(j * W, W), W)
                    left = [operand(j, k) for k in range(slots)]
                    left = jnp.concatenate([jnp.concatenate(pair, axis=0) for pair in left], axis=1)
                    step = 4 * W
                    for m in range(part // step):
                        cols = pl.ds(pl.multiple_of(n * part + m * step, step), step)
                        right = jnp.concatenate([dens[info[j * depth + k], :, cols] for k in range(slots)], axis=0)
                        product = jnp.dot(left, right, preferred_element_type=jnp.float32)
                        product = product.astype(jnp.bfloat16)
                        for s in range(step // W):
                            for p in range(2):
                                half_ref[p, n * (part // W) + m * (step // W) + s, where, :] = product[
                                    p * W : (p + 1) * W, s * W : (s + 1) * W
                                ]

            @pl.when(jnp.logical_not(live(group[0], 2)))
            def _():
                run(2)

            @pl.when(live(group[0], 2))
            def _():
                run(depth)

            return 0

        return lax.fori_loop(0, blocks // H_GROUP, halfway_rows, 0)

    lax.fori_loop(0, PARTS, halfway_part, 0)

    def raw_columns(g, _):
        group = [ranked[g * R_GROUP + t] for t in range(R_GROUP)]

        def run(slots):
            for i in group:
                raw_column(i, slots)

        for slots in range(1, depth + 1):

            @pl.when(info[blocks * depth + group[0]] == slots)
            def _(slots=slots):
                run(slots)

        return 0

    def raw_column(i, slots):
        there = lax.rem(i, HALF)
        side = jnp.bitwise_xor(i // HALF, core)
        right = jnp.concatenate([x for k in range(slots) for x in operand(i, k)], axis=1)
        for m in range(0, HALF, 2):
            rows_of = [side * HALF + lax.rem(there + r, HALF) for r in (m, m + 1)]
            left = [
                jnp.concatenate(
                    [
                        half_ref[p, info[i * depth + k], pl.ds(pl.multiple_of(j * W, W), W), :]
                        for k in range(slots)
                        for p in range(2)
                    ],
                    axis=1,
                )
                for j in rows_of
            ]
            raw = lax.dot_general(
                jnp.concatenate(left, axis=0), right, (((1,), (1,)), ((), ())),
                preferred_element_type=jnp.float32,
            )
            for r, j in zip((m, m + 1), rows_of):
                block = raw[(r - m) * W : (r - m + 1) * W, :]
                if (-r) % HALF < KEEP:
                    q = (-r) % HALF
                    direct[j, q * W : (q + 1) * W, :] = block
                if r < KEEP:
                    turned[i, r * W : (r + 1) * W, :] = block.T

    lax.fori_loop(0, blocks // R_GROUP, raw_columns, 0)

    here = (lax.axis_index("x"), lax.axis_index("z"))
    split = KEEP * W // 2

    def collect(other, _):
        for d in range(4):
            j = 4 * lax.rem(here[0] + d, 4) + other
            outs[d][other] = (direct[j, :split] + turned[j, :split]).astype(jnp.bfloat16)
            j = 4 * other + lax.rem(here[1] + d, 4)
            outs[4 + d][other] = (direct[j, split:] + turned[j, split:]).astype(jnp.bfloat16)
        return 0

    lax.fori_loop(0, 4, collect, 0)


def partial_blocks(info, blocks, depth, *pieces):
    return pl.pallas_call(
        pair_kernel,
        out_shape=[jax.ShapeDtypeStruct((4, KEEP * W // 2, W), jnp.bfloat16)] * 8,
        in_specs=[pl.BlockSpec(memory_space=pltpu.SMEM)] + [pl.BlockSpec(memory_space=pl.ANY)] * len(pieces),
        out_specs=[pl.BlockSpec(memory_space=pltpu.VMEM)] * 8,
        scratch_shapes=[
            pltpu.VMEM((2, blocks, blocks * W, W), jnp.bfloat16),
            pltpu.VMEM((blocks, KEEP * W, W), jnp.float32),
            pltpu.VMEM((blocks, KEEP * W, W), jnp.float32),
            pltpu.VMEM((2, blocks, depth, W, W), jnp.bfloat16),
            pltpu.VMEM((blocks, W, blocks * W), jnp.bfloat16),
            pltpu.SMEM((blocks,), jnp.int32),
            pltpu.SemaphoreType.DMA((len(pieces),)),
            pltpu.SemaphoreType.DMA((PARTS, blocks)),
        ],
        compiler_params=pltpu.CompilerParams(vmem_limit_bytes=58 * 2**20),
        cost_estimate=pl.CostEstimate(flops=13 * 10**9, bytes_accessed=15 * 2**20, transcendentals=0),
        name="pair_blocks",
    )(info, *pieces)


def reorder_kernel(source, target, held, sems):
    copies = [pltpu.make_async_copy(source.at[k], held.at[:, k], sems.at[k]) for k in range(source.shape[0])]
    for copy in copies:
        copy.start()
    for copy in copies:
        copy.wait()
    last = pltpu.make_async_copy(held, target, sems.at[source.shape[0]])
    last.start()
    last.wait()


def by_function(blocks):
    depth, functions = blocks.shape[:2]
    shape = (functions, depth, W, W)
    return pl.pallas_call(
        reorder_kernel,
        out_shape=jax.ShapeDtypeStruct(shape, blocks.dtype),
        in_specs=[pl.BlockSpec(memory_space=pl.ANY)],
        out_specs=pl.BlockSpec(memory_space=pl.ANY),
        scratch_shapes=[pltpu.VMEM(shape, blocks.dtype), pltpu.SemaphoreType.DMA((depth + 1,))],
        cost_estimate=pl.CostEstimate(flops=0, bytes_accessed=4 * 2**20, transcendentals=0),
        name="by_function",
    )(blocks)


def swap_core(pieces):
    return [lax.ppermute(piece, "core", [(0, 1), (1, 0)]) for piece in pieces]


def turn(piece, step):
    return lax.ppermute(piece, "y", [(y, (y + step) % 4) for y in range(4)])


def turn_on(axis, piece, step):
    return lax.ppermute(piece, axis, [(at, (at + step) % 4) for at in range(4)])


def exchange(sets):
    got = {}
    for d in (1, 3, 2):
        for n, (axis, pieces) in enumerate(sets):
            got[n, d] = turn_on(axis, pieces[d], d)
    return [
        pieces[0].astype(jnp.float32) + sum(got[n, d].astype(jnp.float32) for d in (1, 3, 2))
        for n, (_, pieces) in enumerate(sets)
    ]


def ahead(axis, array):
    at = lax.axis_index(axis)
    return [lax.dynamic_index_in_dim(array, (at + d) % 4, 0, keepdims=False) for d in range(4)]


def per_device(three_center, density, pattern, counts, order):
    blocks = pattern.shape[0]
    core = lax.axis_index("core")
    here_y = lax.axis_index("y")
    low, high = density[:W], density[W:]
    low_up, high_down = turn(low, 1), turn(high, -1)
    high_up, low_down = turn(high, 1), turn(low, -1)
    low_far, high_far = turn(low_up, 1), turn(high_down, -1)
    rows = [density, low_up, high_up, low_down, high_down, low_far, high_far]
    info = jnp.concatenate([pattern.reshape(-1), counts]).astype(jnp.int32)
    orb = lax.axis_index("x") * 4 + lax.axis_index("z")
    numbers = jnp.arange(blocks, dtype=jnp.int32)
    inverse = jnp.sum(jnp.where(order[:, None] == numbers[None, :], numbers[:, None], 0), axis=0)
    side = (inverse // HALF) ^ (orb // HALF)
    index = (inverse - orb) % HALF + jnp.where(side == core, 0, HALF)
    index = lax.dynamic_index_in_dim(index.reshape(4, 2, 2), core, 1, keepdims=False)
    index = jnp.take(index, (here_y + jnp.arange(4)) % 4, axis=0, mode="clip").reshape(-1).astype(jnp.int32)
    outgoing = by_function(three_center[0])
    own = lax.all_to_all(outgoing, ("x", "z"), 0, 0, tiled=True)
    first = swap_core([density, low_up, high_down])
    own, first, low_down, high_up, info, index = lax.optimization_barrier((own, first, low_down, high_up, info, index))
    second = swap_core([high_up, low_down])
    other = swap_core(jnp.split(own, 4, axis=0))
    other, second, far = lax.optimization_barrier((other, second, rows[5:]))
    near = [first[0], first[1], second[0], second[1], first[2]] + swap_core(far)
    partial = partial_blocks(info, *pattern.shape, own, *other, *rows, *near)
    first, second = exchange([("x", partial[:4]), ("z", partial[4:])])
    sets = [(axis, [piece.astype(jnp.bfloat16) if d else piece for d, piece in enumerate(ahead(axis, array))])
            for axis, array in (("z", first), ("x", second))]
    kept = jnp.concatenate(exchange(sets), axis=0).reshape(KEEP, W, W)
    mirrored = []
    for q in (3, 2, 1):
        route = []
        for j in range(blocks):
            for c in range(2):
                partner = HALF * ((j // HALF) ^ c) + (j % HALF + q) % HALF
                route.append((j * 2 + c, partner * 2 + c))
        block = lax.ppermute(kept[q], ("x", "z", "core"), route)
        mirrored.append(block.T)
    mine = jnp.concatenate([kept, jnp.stack(mirrored)], axis=0)
    theirs = swap_core(jnp.split(mine, 2, axis=0))
    pool = jnp.concatenate([mine, *theirs], axis=0)
    chunks = [jnp.take(pool, index[2 * d : 2 * d + 2], axis=0, mode="clip") for d in range(4)]
    total = chunks[0]
    for d in (2, 1, 3):
        total = total + turn(chunks[d], d)
    factor = jnp.float32(0.5 / math.sqrt(three_center.shape[2] * lax.axis_size("y") * lax.axis_size("core")))
    return (total * factor).transpose(1, 0, 2).reshape(W, 2 * W)


def solution(mesh):
    fine = Mesh(mesh.devices.reshape(4, 4, 4, 2), ("x", "z", "y", "core"))
    rows, cols = ("x", "z"), ("y", "core")
    return jax.shard_map(
        per_device,
        mesh=fine,
        in_specs=(P(rows, None, cols, None, None), P(cols, None), P(), P(), P()),
        out_specs=P(rows, cols),
        check_vma=False,
    )
```

```python
import functools
import math

import jax
import jax.numpy as jnp
from jax import lax
from jax.experimental import pallas as pl
from jax.experimental.pallas import tpu as pltpu
from jax.sharding import Mesh
from jax.sharding import PartitionSpec as P

W = 128
HALF = 8
KEEP = 5
H_GROUP, R_GROUP = 8, 4
PARTS = 1
SHIFTS = (0, 0, -1, -1, 1, 1, 2, 2)


def pair_kernel(info, *refs):
    pieces, (half_ref, direct, turned, both, dens, ranked, sems, dens_sems) = refs[:-16], refs[-8:]
    outs = refs[-16:-8]
    _, blocks, depth = both.shape[:3]
    core, here_y = lax.axis_index("core"), lax.axis_index("y")

    def live(j, k):
        return info[blocks * depth + j] > k

    def operand(j, k):
        keep = live(j, k).astype(jnp.float32).astype(jnp.bfloat16)
        return [both[p, j, k] * keep for p in range(2)]

    early, first = [], 0
    for piece in pieces:
        if len(piece.shape) == 4:
            p, at = first // blocks, first % blocks
            early.append(pltpu.make_async_copy(piece, both.at[p, pl.ds(at, piece.shape[0])], sems.at[len(early)]))
            first += piece.shape[0]
    rows = []
    for piece in pieces:
        if len(piece.shape) == 2:
            rows += [piece.at[pl.ds(r, W)] for r in range(0, piece.shape[0], W)]
    part = blocks * W // PARTS

    def dens_copy(n, at):
        c, rest = divmod(at, blocks // 2)
        place = 4 * lax.rem(here_y + SHIFTS[rest] + 4, 4) + 2 * jnp.bitwise_xor(core, c) + rest % 2
        cols = pl.ds(pl.multiple_of(n * part, part), part)
        return pltpu.make_async_copy(rows[at].at[:, cols], dens.at[place, :, cols], dens_sems.at[n, at])

    for copy in early:
        copy.start()
    for n in range(PARTS):
        for at in range(blocks):
            dens_copy(n, at).start()

    def place(j, at, slots):
        hit = info[blocks * depth + j] == slots

        @pl.when(hit)
        def _():
            ranked[at] = j

        return at + hit.astype(jnp.int32)

    filled = 0
    for slots in range(depth, 0, -1):
        filled = lax.fori_loop(0, blocks, functools.partial(place, slots=slots), filled)
    for copy in early:
        copy.wait()

    def halfway_part(n, _):
        for at in range(blocks):
            dens_copy(n, at).wait()

        def halfway_rows(g, _):
            group = [ranked[g * H_GROUP + t] for t in range(H_GROUP)]

            def run(slots):
                for j in group:
                    where = pl.ds(pl.multiple_of(j * W, W), W)
                    left = [operand(j, k) for k in range(slots)]
                    left = jnp.concatenate([jnp.concatenate(pair, axis=0) for pair in left], axis=1)
                    step = 4 * W
                    for m in range(part // step):
                        cols = pl.ds(pl.multiple_of(n * part + m * step, step), step)
                        right = jnp.concatenate([dens[info[j * depth + k], :, cols] for k in range(slots)], axis=0)
                        product = jnp.dot(left, right, preferred_element_type=jnp.float32)
                        product = product.astype(jnp.bfloat16)
                        for s in range(step // W):
                            for p in range(2):
                                half_ref[p, n * (part // W) + m * (step // W) + s, where, :] = product[
                                    p * W : (p + 1) * W, s * W : (s + 1) * W
                                ]

            @pl.when(jnp.logical_not(live(group[0], 2)))
            def _():
                run(2)

            @pl.when(live(group[0], 2))
            def _():
                run(depth)

            return 0

        return lax.fori_loop(0, blocks // H_GROUP, halfway_rows, 0)

    lax.fori_loop(0, PARTS, halfway_part, 0)

    def raw_columns(g, _):
        group = [ranked[g * R_GROUP + t] for t in range(R_GROUP)]

        def run(slots):
            for i in group:
                raw_column(i, slots)

        for slots in range(1, depth + 1):

            @pl.when(info[blocks * depth + group[0]] == slots)
            def _(slots=slots):
                run(slots)

        return 0

    def raw_column(i, slots):
        there = lax.rem(i, HALF)
        side = jnp.bitwise_xor(i // HALF, core)
        right = jnp.concatenate([x for k in range(slots) for x in operand(i, k)], axis=1)
        for m in range(0, HALF, 2):
            rows_of = [side * HALF + lax.rem(there + r, HALF) for r in (m, m + 1)]
            left = [
                jnp.concatenate(
                    [
                        half_ref[p, info[i * depth + k], pl.ds(pl.multiple_of(j * W, W), W), :]
                        for k in range(slots)
                        for p in range(2)
                    ],
                    axis=1,
                )
                for j in rows_of
            ]
            raw = lax.dot_general(
                jnp.concatenate(left, axis=0), right, (((1,), (1,)), ((), ())),
                preferred_element_type=jnp.float32,
            )
            for r, j in zip((m, m + 1), rows_of):
                block = raw[(r - m) * W : (r - m + 1) * W, :]
                if (-r) % HALF < KEEP:
                    q = (-r) % HALF
                    direct[j, q * W : (q + 1) * W, :] = block
                if r < KEEP:
                    turned[i, r * W : (r + 1) * W, :] = block.T

    lax.fori_loop(0, blocks // R_GROUP, raw_columns, 0)

    here = (lax.axis_index("x"), lax.axis_index("z"))
    split = KEEP * W // 2

    def collect(other, _):
        for d in range(4):
            j = 4 * lax.rem(here[0] + d, 4) + other
            outs[d][other] = (direct[j, :split] + turned[j, :split]).astype(jnp.bfloat16)
            j = 4 * other + lax.rem(here[1] + d, 4)
            outs[4 + d][other] = (direct[j, split:] + turned[j, split:]).astype(jnp.bfloat16)
        return 0

    lax.fori_loop(0, 4, collect, 0)


def partial_blocks(info, blocks, depth, *pieces):
    return pl.pallas_call(
        pair_kernel,
        out_shape=[jax.ShapeDtypeStruct((4, KEEP * W // 2, W), jnp.bfloat16)] * 8,
        in_specs=[pl.BlockSpec(memory_space=pltpu.SMEM)] + [pl.BlockSpec(memory_space=pl.ANY)] * len(pieces),
        out_specs=[pl.BlockSpec(memory_space=pltpu.VMEM)] * 8,
        scratch_shapes=[
            pltpu.VMEM((2, blocks, blocks * W, W), jnp.bfloat16),
            pltpu.VMEM((blocks, KEEP * W, W), jnp.float32),
            pltpu.VMEM((blocks, KEEP * W, W), jnp.float32),
            pltpu.VMEM((2, blocks, depth, W, W), jnp.bfloat16),
            pltpu.VMEM((blocks, W, blocks * W), jnp.bfloat16),
            pltpu.SMEM((blocks,), jnp.int32),
            pltpu.SemaphoreType.DMA((len(pieces),)),
            pltpu.SemaphoreType.DMA((PARTS, blocks)),
        ],
        compiler_params=pltpu.CompilerParams(vmem_limit_bytes=58 * 2**20),
        cost_estimate=pl.CostEstimate(flops=13 * 10**9, bytes_accessed=15 * 2**20, transcendentals=0),
        name="pair_blocks",
    )(info, *pieces)


def reorder_kernel(source, target, held, sems):
    depth = source.shape[0]
    into = [pltpu.make_async_copy(source.at[k], held.at[k], sems.at[k]) for k in range(depth)]
    out = [pltpu.make_async_copy(held.at[k], target.at[:, k], sems.at[depth + k]) for k in range(depth)]
    for copy in into:
        copy.start()
    for arrived, copy in zip(into, out):
        arrived.wait()
        copy.start()
    for copy in out:
        copy.wait()


def by_function(blocks):
    depth, functions = blocks.shape[:2]
    shape = (functions, depth, W, W)
    return pl.pallas_call(
        reorder_kernel,
        out_shape=jax.ShapeDtypeStruct(shape, blocks.dtype),
        in_specs=[pl.BlockSpec(memory_space=pl.ANY)],
        out_specs=pl.BlockSpec(memory_space=pl.ANY),
        scratch_shapes=[pltpu.VMEM(blocks.shape, blocks.dtype), pltpu.SemaphoreType.DMA((2 * depth,))],
        cost_estimate=pl.CostEstimate(flops=0, bytes_accessed=4 * 2**20, transcendentals=0),
        name="by_function",
    )(blocks)


def swap_core(pieces):
    return [lax.ppermute(piece, "core", [(0, 1), (1, 0)]) for piece in pieces]


def turn(piece, step):
    return lax.ppermute(piece, "y", [(y, (y + step) % 4) for y in range(4)])


def turn_on(axis, piece, step):
    return lax.ppermute(piece, axis, [(at, (at + step) % 4) for at in range(4)])


def exchange(sets):
    got = {}
    for d in (1, 3, 2):
        for n, (axis, pieces) in enumerate(sets):
            got[n, d] = turn_on(axis, pieces[d], d)
    return [
        pieces[0].astype(jnp.float32) + sum(got[n, d].astype(jnp.float32) for d in (1, 3, 2))
        for n, (_, pieces) in enumerate(sets)
    ]


def ahead(axis, array):
    at = lax.axis_index(axis)
    return [lax.dynamic_index_in_dim(array, (at + d) % 4, 0, keepdims=False) for d in range(4)]


def per_device(three_center, density, pattern, counts, order):
    blocks = pattern.shape[0]
    core = lax.axis_index("core")
    here_y = lax.axis_index("y")
    low, high = density[:W], density[W:]
    low_up, high_down = turn(low, 1), turn(high, -1)
    high_up, low_down = turn(high, 1), turn(low, -1)
    low_far, high_far = turn(low_up, 1), turn(high_down, -1)
    rows = [density, low_up, high_up, low_down, high_down, low_far, high_far]
    info = jnp.concatenate([pattern.reshape(-1), counts]).astype(jnp.int32)
    orb = lax.axis_index("x") * 4 + lax.axis_index("z")
    numbers = jnp.arange(blocks, dtype=jnp.int32)
    inverse = jnp.sum(jnp.where(order[:, None] == numbers[None, :], numbers[:, None], 0), axis=0)
    side = (inverse // HALF) ^ (orb // HALF)
    index = (inverse - orb) % HALF + jnp.where(side == core, 0, HALF)
    index = lax.dynamic_index_in_dim(index.reshape(4, 2, 2), core, 1, keepdims=False)
    index = jnp.take(index, (here_y + jnp.arange(4)) % 4, axis=0, mode="clip").reshape(-1).astype(jnp.int32)
    outgoing = by_function(three_center[0])
    own = lax.all_to_all(outgoing, ("x", "z"), 0, 0, tiled=True)
    first = swap_core([density, low_up, high_down])
    own, first, low_down, high_up, info, index = lax.optimization_barrier((own, first, low_down, high_up, info, index))
    second = swap_core([high_up, low_down])
    other = swap_core(jnp.split(own, 4, axis=0))
    other, second, far = lax.optimization_barrier((other, second, rows[5:]))
    near = [first[0], first[1], second[0], second[1], first[2]] + swap_core(far)
    partial = partial_blocks(info, *pattern.shape, own, *other, *rows, *near)
    first, second = exchange([("x", partial[:4]), ("z", partial[4:])])
    sets = [(axis, [piece.astype(jnp.bfloat16) if d else piece for d, piece in enumerate(ahead(axis, array))])
            for axis, array in (("z", first), ("x", second))]
    kept = jnp.concatenate(exchange(sets), axis=0).reshape(KEEP, W, W)
    mirrored = []
    for q in (3, 2, 1):
        route = []
        for j in range(blocks):
            for c in range(2):
                partner = HALF * ((j // HALF) ^ c) + (j % HALF + q) % HALF
                route.append((j * 2 + c, partner * 2 + c))
        block = lax.ppermute(kept[q], ("x", "z", "core"), route)
        mirrored.append(block.T)
    mine = jnp.concatenate([kept, jnp.stack(mirrored)], axis=0)
    theirs = swap_core(jnp.split(mine, 2, axis=0))
    pool = jnp.concatenate([mine, *theirs], axis=0)
    chunks = [jnp.take(pool, index[2 * d : 2 * d + 2], axis=0, mode="clip") for d in range(4)]
    total = chunks[0]
    for d in (2, 1, 3):
        total = total + turn(chunks[d], d)
    factor = jnp.float32(0.5 / math.sqrt(three_center.shape[2] * lax.axis_size("y") * lax.axis_size("core")))
    return (total * factor).transpose(1, 0, 2).reshape(W, 2 * W)


def solution(mesh):
    fine = Mesh(mesh.devices.reshape(4, 4, 4, 2), ("x", "z", "y", "core"))
    rows, cols = ("x", "z"), ("y", "core")
    return jax.shard_map(
        per_device,
        mesh=fine,
        in_specs=(P(rows, None, cols, None, None), P(cols, None), P(), P(), P()),
        out_specs=P(rows, cols),
        check_vma=False,
    )
```
